128 devices in a mesh: dp: 16 (over y, z), ctx: 8 (over x, core).
Axes of the slice: x: 4, y: 4, z: 4, core: 2. Of those that a mesh axis runs over, the one named last changes fastest.
Arguments:
- tokens: bfloat16 [32, 8192, 1280], P('dp', 'ctx'), may hold values from -16.77051 to 16.77051
- slot_param: bfloat16 [1280, 64], replicated, may hold values from -1 to 1
- w_in: bfloat16 [64, 1280, 5120], P('dp', None, 'ctx'), may hold values from -6 to 6
- w_out: bfloat16 [64, 5120, 1280], P('dp', 'ctx'), may hold values from -0.3125 to 0.3125
Outputs:
- mixed: bfloat16 [32, 8192, 1280], P('dp', 'ctx')
The draws below stay inside these ranges and needn't reach their ends.
All inputs are finite; a program needn't handle non-finite values.
Results may differ from the reference program's by a relative error of at most 0.013.
Values may be sent and summed in bfloat16 or wider, within the bound.
No kernel may reach another device: no remote copies, remote signals or barrier semaphores. Data moves between devices by JAX's collectives and lax.ppermute only.
A program may use at most 64 MiB of HBM per device.

```python
import jax
import jax.numpy as jnp
from jax import lax

D = 1280
FF = 5120
EXPERTS = 64
SLOTS = 64
TOKENS = 8192
CLIPS = 32


def slot_signs(key):
    flips = jax.random.bernoulli(key, 0.5, (D, SLOTS))
    return jnp.where(flips, 1.0, -1.0).astype(jnp.float32)


def draw_slot_param(key, part):
    signs = slot_signs(key)
    return (signs * D ** (-0.5)).astype(jnp.bfloat16)


def draw_tokens(key, part):
    key = jax.random.fold_in(key, 11)
    base_key = jax.random.fold_in(key, 0)
    shape = (CLIPS, TOKENS, D)
    values = jax.random.truncated_normal(base_key, -6.0, 6.0, shape, jnp.float32)
    return values.astype(jnp.bfloat16)


def block_scale(key, shape, pieces, low, largest):
    gain = 1.0
    for dim, parts in pieces:
        steps = jax.random.uniform(jax.random.fold_in(jax.random.fold_in(key, 6), dim), (parts,), jnp.float32, low / len(pieces), largest / len(pieces))
        gain = gain * jnp.repeat(jnp.exp(steps), shape[dim] // parts).reshape((-1,) + (1,) * (len(shape) - 1 - dim))
    return gain


def gaussian(rng, extent, deviation, most, cuts=(), held_as=jnp.bfloat16):
    gain = block_scale(rng, extent, cuts, -0.22, 0.18) if cuts else 1.0
    drawn = jax.random.normal(rng, extent, jnp.float32) * deviation * gain
    return jnp.minimum(jnp.maximum(drawn, -most), most).astype(held_as)


def setup_inputs(seed: int = 0) -> dict:
    arg_keys = jax.random.split(jax.random.key(seed), 5)
    return {
        "tokens": draw_tokens(jax.random.fold_in(arg_keys[4], 71), 0),
        "slot_param": draw_slot_param(jax.random.fold_in(arg_keys[4], 71), 0),
        "w_in": gaussian(arg_keys[2], (EXPERTS, D, FF), 1 ** -0.5, 6.0, ((0, 16), (2, 8))),
        "w_out": gaussian(arg_keys[3], (EXPERTS, FF, D), (FF // 16) ** -0.5, 0.3125, ((0, 16), (1, 8))),
    }


def clip_logits(clip_tokens, slot_param):
    return jnp.dot(slot_param.T, clip_tokens.T, preferred_element_type=jnp.float32)


def clip_slots(clip_tokens, slot_param):
    logits = clip_logits(clip_tokens, slot_param)
    peak = jnp.max(logits, axis=1, keepdims=True)
    expd = jnp.exp(logits - peak)
    total = jnp.sum(expd, axis=1, keepdims=True)
    dispatch = expd.astype(jnp.bfloat16)
    gathered = jnp.dot(dispatch, clip_tokens, preferred_element_type=jnp.float32)
    return (gathered / total).astype(jnp.bfloat16)


def one_expert(packed):
    inputs, first, second = packed
    pre = jnp.dot(inputs, first, preferred_element_type=jnp.float32)
    hidden = jax.nn.gelu(pre, approximate=False).astype(jnp.bfloat16)
    return jnp.dot(hidden, second, preferred_element_type=jnp.float32).astype(jnp.bfloat16)


def clip_mix(packed, slot_param):
    clip_tokens, outputs = packed
    logits = clip_logits(clip_tokens, slot_param)
    row_top = jnp.max(logits, axis=0, keepdims=True)
    expd = jnp.exp(logits - row_top)
    combine = (expd / jnp.sum(expd, axis=0, keepdims=True)).astype(jnp.bfloat16)
    return jnp.dot(combine.T, outputs, preferred_element_type=jnp.float32).astype(jnp.bfloat16)


def reference(tokens, slot_param, w_in, w_out):
    slot_in = lax.map(lambda clip_tokens: clip_slots(clip_tokens, slot_param), tokens)
    by_expert = jnp.transpose(slot_in, (1, 0, 2))
    expert_out = lax.map(one_expert, (by_expert, w_in, w_out))
    outputs = jnp.transpose(expert_out, (1, 0, 2))
    return lax.map(lambda packed: clip_mix(packed, slot_param), (tokens, outputs))
```

```python
import functools

import jax
import jax.numpy as jnp
import numpy as np
from jax import lax
from jax.experimental import pallas as pl
from jax.experimental.pallas import tpu as pltpu
from jax.sharding import PartitionSpec as P

F32 = jnp.float32
BF16 = jnp.bfloat16
HALF = 640
WIDE = HALF + 128
NT = (((1,), (1,)), ((), ()))


def with_stats(values, peak, high, low):
    lane = lax.broadcasted_iota(jnp.int32, (values.shape[0], 128), 1)
    stats = jnp.where(lane == 0, peak, jnp.where(lane == 1, high, jnp.where(lane == 2, low, 0.0)))
    return jnp.concatenate([values, stats], axis=1)


def split_total(total):
    high = total.astype(BF16).astype(F32)
    return high, total - high


def gather_kernel(pieces, tokens_hbm, slots_ref, send_ref, keep_ref, logits_ref, tokens, whole, sems):
    core = lax.axis_index("core")
    mine = pl.ds(pl.multiple_of(core * HALF, 128), HALF)
    other = pl.ds(pl.multiple_of((1 - core) * HALF, 128), HALF)
    clips, count, _ = tokens.shape
    step = count // pieces

    def copy(b, i):
        rows = pl.ds(i * step, step)
        return pltpu.make_async_copy(tokens_hbm.at[b, rows], tokens.at[b, rows], sems.at[b, i])

    for b in range(clips):
        for i in range(pieces):
            copy(b, i).start()
    for b in range(clips):
        for i in range(pieces):
            copy(b, i).wait()
            logits_ref[b, :, pl.ds(i * step, step)] = lax.dot_general(
                slots_ref[...], tokens[b, pl.ds(i * step, step), :], NT, preferred_element_type=F32
            )
        logits = logits_ref[b]
        peak = jnp.max(logits, axis=1, keepdims=True).astype(BF16).astype(F32)
        expd = jnp.exp(logits - peak)
        total = jnp.sum(expd, axis=1, keepdims=True)
        whole[...] = jnp.dot(expd.astype(BF16), tokens[b], preferred_element_type=F32)
        high, low = split_total(total)
        send_ref[b] = with_stats(whole[:, other], peak, high, low).astype(BF16)
        keep_ref[b] = with_stats(whole[:, mine], peak, total, jnp.zeros_like(total))


def gather(tokens, slots_t):
    clips, count, width = tokens.shape
    slots = slots_t.shape[0]
    pieces = 4
    return pl.pallas_call(
        functools.partial(gather_kernel, pieces),
        out_shape=[
            jax.ShapeDtypeStruct((clips, slots, WIDE), BF16),
            jax.ShapeDtypeStruct((clips, slots, WIDE), F32),
            jax.ShapeDtypeStruct((clips, slots, count), F32),
        ],
        in_specs=[pl.BlockSpec(memory_space=pl.ANY), pl.BlockSpec(memory_space=pltpu.VMEM)],
        out_specs=[pl.BlockSpec(memory_space=pltpu.VMEM)] * 3,
        scratch_shapes=[
            pltpu.VMEM((clips, count, width), BF16),
            pltpu.VMEM((slots, width), F32),
            pltpu.SemaphoreType.DMA((clips, pieces)),
        ],
        compiler_params=pltpu.CompilerParams(vmem_limit_bytes=40 << 20),
        cost_estimate=pl.CostEstimate(
            flops=4 * clips * slots * count * width,
            bytes_accessed=2 * clips * count * width,
            transcendentals=clips * slots * count,
        ),
        name="gather",
    )(tokens, slots_t)


def pack_kernel(keep_ref, recv_ref, out_ref):
    halves = []
    for b in range(2):
        kept, got = keep_ref[b], recv_ref[b].astype(F32)
        peak_k, peak_g = kept[:, HALF : HALF + 1], got[:, HALF : HALF + 1]
        peak = jnp.maximum(peak_k, peak_g)
        scale_k, scale_g = jnp.exp(peak_k - peak), jnp.exp(peak_g - peak)
        total = scale_k * kept[:, HALF + 1 : HALF + 2] + scale_g * (
            got[:, HALF + 1 : HALF + 2] + got[:, HALF + 2 : HALF + 3]
        )
        value = scale_k * kept[:, :HALF] + scale_g * got[:, :HALF]
        halves.append(with_stats(value, peak, *split_total(total)).reshape(8, 8, WIDE))
    first, second = halves
    top = lax.broadcasted_iota(jnp.int32, first.shape, 1) < 4
    even = jnp.where(top, first, pltpu.roll(second, 4, 1)).astype(BF16)
    odd = jnp.where(top, pltpu.roll(first, 4, 1), second).astype(BF16)
    for j in range(8):
        for x in range(4):
            out_ref[8 * j + x] = even[j]
            out_ref[8 * j + 4 + x] = odd[j]


def pack(keep, recv):
    return pl.pallas_call(
        pack_kernel,
        out_shape=jax.ShapeDtypeStruct((64, 8, WIDE), BF16),
        compiler_params=pltpu.CompilerParams(vmem_limit_bytes=24 << 20),
        name="pack",
    )(keep, recv)


def expert_kernel(own_ref, oth_ref, w_in_hbm, w_out_hbm, send_ref, keep_ref, w_in, w_out, inputs, pre, out, sems):
    core = lax.axis_index("core")
    mine = pl.ds(pl.multiple_of(core * HALF, 128), HALF)
    other = pl.ds(pl.multiple_of((1 - core) * HALF, 128), HALF)
    experts = w_in.shape[0]
    copies_in = [pltpu.make_async_copy(w_in_hbm.at[e], w_in.at[e], sems.at[0, e]) for e in range(experts)]
    copies_out = [pltpu.make_async_copy(w_out_hbm.at[e], w_out.at[e], sems.at[1, e]) for e in range(experts)]
    for copy in copies_in + copies_out:
        copy.start()
    for i in range(8):
        own = own_ref[8 * i : 8 * i + 8].astype(F32).reshape(2, 4, 8, WIDE)
        oth = oth_ref[8 * i : 8 * i + 8, :, :HALF].astype(F32).reshape(2, 4, 8, HALF)
        peaks = own[..., HALF : HALF + 1]
        weight = jnp.exp(peaks - jnp.max(peaks, axis=1, keepdims=True))
        total = jnp.sum(weight * (own[..., HALF + 1 : HALF + 2] + own[..., HALF + 2 : HALF + 3]), axis=1, keepdims=True)
        weight = weight / total
        rows = pl.ds(16 * i, 16)
        inputs[rows, mine] = jnp.sum(weight * own[..., :HALF], axis=1).reshape(16, HALF).astype(BF16)
        inputs[rows, other] = jnp.sum(weight * oth, axis=1).reshape(16, HALF).astype(BF16)
    slot = lax.broadcasted_iota(jnp.int32, (128, 1), 0) % 4
    for e in range(experts):
        copies_in[e].wait()
        here = jnp.dot(inputs[...], w_in[e], preferred_element_type=F32)
        pre[...] = here if e == 0 else jnp.where(slot == e, here, pre[...])
    value = pre[...]
    hidden = (0.5 * value * (1.0 + lax.erf(value * np.float32(np.sqrt(0.5))))).astype(BF16)
    for e in range(experts):
        copies_out[e].wait()
        here = jnp.dot(hidden, w_out[e], preferred_element_type=F32)
        out[...] = here if e == 0 else jnp.where(slot == e, here, out[...])
    send_ref[...] = out[:, other].astype(BF16)
    keep_ref[...] = out[:, mine]


def expert(own, oth, w_in, w_out):
    experts, width, hidden = w_in.shape
    vmem = pl.BlockSpec(memory_space=pltpu.VMEM)
    hbm = pl.BlockSpec(memory_space=pl.ANY)
    return pl.pallas_call(
        expert_kernel,
        out_shape=[jax.ShapeDtypeStruct((128, HALF), BF16), jax.ShapeDtypeStruct((128, HALF), F32)],
        in_specs=[vmem, vmem, hbm, hbm],
        out_specs=[vmem, vmem],
        scratch_shapes=[
            pltpu.VMEM(w_in.shape, BF16),
            pltpu.VMEM(w_out.shape, BF16),
            pltpu.VMEM((128, width), BF16),
            pltpu.VMEM((128, hidden), F32),
            pltpu.VMEM((128, width), F32),
            pltpu.SemaphoreType.DMA((2, experts)),
        ],
        compiler_params=pltpu.CompilerParams(vmem_limit_bytes=48 << 20),
        name="expert",
    )(own, oth, w_in, w_out)


def combine_kernel(logits_ref, out_ref):
    for b in range(2):
        logits = logits_ref[b]
        expd = jnp.exp(logits - jnp.max(logits, axis=0, keepdims=True))
        combine = expd / jnp.sum(expd, axis=0, keepdims=True)
        out_ref[b] = combine.T.astype(BF16)


def combine(logits):
    clips, slots, count = logits.shape
    return pl.pallas_call(
        combine_kernel,
        out_shape=jax.ShapeDtypeStruct((clips, count, slots), BF16),
        compiler_params=pltpu.CompilerParams(vmem_limit_bytes=24 << 20),
        cost_estimate=pl.CostEstimate(flops=8 * logits.size, bytes_accessed=6 * logits.size, transcendentals=logits.size),
        name="combine",
    )(logits)


def mix_kernel(combine_ref, own_ref, oth_ref, out_ref, outputs):
    @pl.when((pl.program_id(0) == 0) & (pl.program_id(1) == 0))
    def _():
        core = lax.axis_index("core")
        mine = pl.ds(pl.multiple_of(core * HALF, 128), HALF)
        other = pl.ds(pl.multiple_of((1 - core) * HALF, 128), HALF)
        top = lax.broadcasted_iota(jnp.int32, (2, 8, HALF), 1) < 4
        for ref, lanes in ((own_ref, mine), (oth_ref, other)):
            for i in range(4):
                part = ref[16 * i : 16 * i + 16].astype(F32).reshape(4, 4, 8, HALF)
                part = jnp.sum(part, axis=1).reshape(2, 2, 8, HALF)
                even, odd = part[:, 0], part[:, 1]
                first = jnp.where(top, even, pltpu.roll(odd, 4, 1))
                second = jnp.where(top, pltpu.roll(even, 4, 1), odd)
                rows = pl.ds(16 * i, 16)
                outputs[0, rows, lanes] = first.reshape(16, HALF).astype(BF16)
                outputs[1, rows, lanes] = second.reshape(16, HALF).astype(BF16)

    mixed = jnp.dot(combine_ref[0], outputs[pl.program_id(0)], preferred_element_type=F32)
    out_ref[0] = mixed.astype(BF16)


def mix(weights, own, oth):
    clips, count, slots = weights.shape
    rows = 512
    width = 2 * HALF
    return pl.pallas_call(
        mix_kernel,
        out_shape=jax.ShapeDtypeStruct((clips, count, width), BF16),
        grid=(clips, count // rows),
        in_specs=[
            pl.BlockSpec((1, rows, slots), lambda b, i: (b, i, 0)),
            pl.BlockSpec(own.shape, lambda b, i: (0, 0, 0)),
            pl.BlockSpec(own.shape, lambda b, i: (0, 0, 0)),
        ],
        out_specs=pl.BlockSpec((1, rows, width), lambda b, i: (b, i, 0)),
        scratch_shapes=[pltpu.VMEM((clips, slots, width), BF16)],
        compiler_params=pltpu.CompilerParams(vmem_limit_bytes=32 << 20),
        name="mix",
    )(weights, own, oth)


def swap(x):
    return lax.ppermute(x, "core", [(0, 1), (1, 0)])


def exchange(x):
    return lax.all_to_all(x, ("dp", "x"), 0, 0, tiled=True)


def on_device(tokens, slot_param, w_in, w_out):
    send, keep, logits = gather(tokens, slot_param.T)
    own = exchange(pack(keep, swap(send)))
    weights = combine(logits)
    send, keep = expert(own, swap(own), w_in, w_out)
    summed = (keep + swap(send).astype(F32)).astype(BF16).reshape(16, 1, 8, HALF)
    own = exchange(jnp.broadcast_to(summed, (16, 4, 8, HALF)).reshape(64, 8, HALF))
    return mix(weights, own, swap(own))


def solution(mesh):
    ctx = ("x", "core")
    split = jax.sharding.Mesh(np.asarray(mesh.devices).reshape(16, 4, 2), ("dp",) + ctx)
    placed = (P("dp", ctx, None), P(), P("dp", None, ctx), P("dp", ctx, None))
    return jax.shard_map(
        on_device, mesh=split, in_specs=placed, out_specs=P("dp", ctx, None), check_vma=False
    )
```

```python
import functools

import jax
import jax.numpy as jnp
import numpy as np
from jax import lax
from jax.experimental import pallas as pl
from jax.experimental.pallas import tpu as pltpu
from jax.sharding import PartitionSpec as P

F32 = jnp.float32
BF16 = jnp.bfloat16
HALF = 640
WIDE = HALF + 128
NT = (((1,), (1,)), ((), ()))


def with_stats(values, peak, high, low):
    lane = lax.broadcasted_iota(jnp.int32, (values.shape[0], 128), 1)
    stats = jnp.where(lane == 0, peak, jnp.where(lane == 1, high, jnp.where(lane == 2, low, 0.0)))
    return jnp.concatenate([values, stats], axis=1)


def split_total(total):
    high = total.astype(BF16).astype(F32)
    return high, total - high


def gather_kernel(pieces, tokens_hbm, slots_hbm, send_ref, keep_ref, logits_ref, tokens, slots_ref, whole, sems):
    core = lax.axis_index("core")
    mine = pl.ds(pl.multiple_of(core * HALF, 128), HALF)
    other = pl.ds(pl.multiple_of((1 - core) * HALF, 128), HALF)
    clips, count, _ = tokens.shape
    step = count // pieces

    def copy(b, i):
        rows = pl.ds(i * step, step)
        return pltpu.make_async_copy(tokens_hbm.at[b, rows], tokens.at[b, rows], sems.at[b, i])

    slots_copy = pltpu.make_async_copy(slots_hbm, slots_ref, sems.at[clips, 0])
    slots_copy.start()
    for b in range(clips):
        for i in range(pieces):
            copy(b, i).start()
    slots_copy.wait()
    for b in range(clips):
        for i in range(pieces):
            copy(b, i).wait()
            logits_ref[b, :, pl.ds(i * step, step)] = lax.dot_general(
                slots_ref[...], tokens[b, pl.ds(i * step, step), :], NT, preferred_element_type=F32
            )
        logits = logits_ref[b]
        peak = jnp.max(logits, axis=1, keepdims=True).astype(BF16).astype(F32)
        expd = jnp.exp(logits - peak)
        total = jnp.sum(expd, axis=1, keepdims=True)
        whole[...] = jnp.dot(expd.astype(BF16), tokens[b], preferred_element_type=F32)
        high, low = split_total(total)
        send_ref[b] = with_stats(whole[:, other], peak, high, low).astype(BF16)
        keep_ref[b] = with_stats(whole[:, mine], peak, total, jnp.zeros_like(total))


def gather(tokens, slots_t):
    clips, count, width = tokens.shape
    slots = slots_t.shape[0]
    pieces = 2
    return pl.pallas_call(
        functools.partial(gather_kernel, pieces),
        out_shape=[
            pltpu.VMEM((clips, slots, WIDE), BF16),
            pltpu.VMEM((clips, slots, WIDE), F32),
            pltpu.VMEM((clips, slots, count), F32),
        ],
        in_specs=[pl.BlockSpec(memory_space=pl.ANY)] * 2,
        out_specs=[pl.BlockSpec(memory_space=pltpu.VMEM)] * 3,
        scratch_shapes=[
            pltpu.VMEM((clips, count, width), BF16),
            pltpu.VMEM((slots, width), BF16),
            pltpu.VMEM((slots, width), F32),
            pltpu.SemaphoreType.DMA((clips + 1, pieces)),
        ],
        compiler_params=pltpu.CompilerParams(vmem_limit_bytes=62 << 20),
        cost_estimate=pl.CostEstimate(
            flops=4 * clips * slots * count * width,
            bytes_accessed=2 * clips * count * width,
            transcendentals=clips * slots * count,
        ),
        name="gather",
    )(tokens, slots_t)


def pack_kernel(keep_ref, recv_ref, out_ref):
    halves = []
    for b in range(2):
        kept, got = keep_ref[b], recv_ref[b].astype(F32)
        peak_k, peak_g = kept[:, HALF : HALF + 1], got[:, HALF : HALF + 1]
        peak = jnp.maximum(peak_k, peak_g)
        scale_k, scale_g = jnp.exp(peak_k - peak), jnp.exp(peak_g - peak)
        total = scale_k * kept[:, HALF + 1 : HALF + 2] + scale_g * (
            got[:, HALF + 1 : HALF + 2] + got[:, HALF + 2 : HALF + 3]
        )
        value = scale_k * kept[:, :HALF] + scale_g * got[:, :HALF]
        halves.append(with_stats(value, peak, *split_total(total)).reshape(8, 8, WIDE))
    first, second = halves
    top = lax.broadcasted_iota(jnp.int32, first.shape, 1) < 4
    even = jnp.where(top, first, pltpu.roll(second, 4, 1)).astype(BF16)
    odd = jnp.where(top, pltpu.roll(first, 4, 1), second).astype(BF16)
    for j in range(8):
        for x in range(4):
            out_ref[8 * j + x] = even[j]
            out_ref[8 * j + 4 + x] = odd[j]


def pack(keep, recv):
    return pl.pallas_call(
        pack_kernel,
        out_shape=jax.ShapeDtypeStruct((64, 8, WIDE), BF16),
        compiler_params=pltpu.CompilerParams(vmem_limit_bytes=24 << 20),
        cost_estimate=pl.CostEstimate(flops=1 << 36, bytes_accessed=100 << 20, transcendentals=0),
        name="pack",
    )(keep, recv)


def reduce_kernel(parts_ref, out_ref):
    for i in range(8):
        part = parts_ref[8 * i : 8 * i + 8].astype(F32).reshape(2, 4, 8, WIDE)
        peak = part[..., HALF : HALF + 1]
        weight = jnp.exp(peak - jnp.max(peak, axis=1, keepdims=True))
        total = weight * (part[..., HALF + 1 : HALF + 2] + part[..., HALF + 2 : HALF + 3])
        weight = weight / jnp.sum(total, axis=1, keepdims=True)
        slot_in = jnp.sum(weight * part[..., :HALF], axis=1)
        out_ref[pl.ds(16 * i, 16), :] = slot_in.reshape(16, HALF).astype(BF16)


def reduce(parts):
    return pl.pallas_call(
        reduce_kernel,
        out_shape=jax.ShapeDtypeStruct((128, HALF), BF16),
        compiler_params=pltpu.CompilerParams(vmem_limit_bytes=24 << 20),
        name="reduce",
    )(parts)


def expert_kernel(own_ref, oth_ref, w_in, w_out, send_ref, keep_ref, inputs, pre, out):
    core = lax.axis_index("core")
    mine = pl.ds(pl.multiple_of(core * HALF, 128), HALF)
    other = pl.ds(pl.multiple_of((1 - core) * HALF, 128), HALF)
    experts = w_in.shape[0]
    inputs[:, mine] = own_ref[...]
    inputs[:, other] = oth_ref[...]
    slot = lax.broadcasted_iota(jnp.int32, (128, 1), 0) % 4
    for e in range(experts):
        here = jnp.dot(inputs[...], w_in[e], preferred_element_type=F32)
        pre[...] = here if e == 0 else jnp.where(slot == e, here, pre[...])
    value = pre[...]
    hidden = (0.5 * value * (1.0 + lax.erf(value * np.float32(np.sqrt(0.5))))).astype(BF16)
    for e in range(experts):
        here = jnp.dot(hidden, w_out[e], preferred_element_type=F32)
        out[...] = here if e == 0 else jnp.where(slot == e, here, out[...])
    send_ref[...] = out[:, other].astype(BF16)
    keep_ref[...] = out[:, mine]


def expert(own, oth, w_in, w_out):
    experts, width, hidden = w_in.shape
    vmem = pl.BlockSpec(memory_space=pltpu.VMEM)
    return pl.pallas_call(
        expert_kernel,
        out_shape=[jax.ShapeDtypeStruct((128, HALF), BF16), jax.ShapeDtypeStruct((128, HALF), F32)],
        in_specs=[vmem] * 4,
        out_specs=[vmem, vmem],
        scratch_shapes=[
            pltpu.VMEM((128, width), BF16),
            pltpu.VMEM((128, hidden), F32),
            pltpu.VMEM((128, width), F32),
        ],
        compiler_params=pltpu.CompilerParams(vmem_limit_bytes=24 << 20),
        name="expert",
    )(own, oth, w_in, w_out)


def combine_kernel(logits_ref, out_ref):
    for b in range(2):
        logits = logits_ref[b]
        expd = jnp.exp(logits - jnp.max(logits, axis=0, keepdims=True))
        combine = expd / jnp.sum(expd, axis=0, keepdims=True)
        out_ref[b] = combine.T.astype(BF16)


def combine(logits):
    clips, slots, count = logits.shape
    return pl.pallas_call(
        combine_kernel,
        out_shape=jax.ShapeDtypeStruct((clips, count, slots), BF16),
        compiler_params=pltpu.CompilerParams(vmem_limit_bytes=24 << 20),
        cost_estimate=pl.CostEstimate(flops=8 * logits.size, bytes_accessed=6 * logits.size, transcendentals=logits.size),
        name="combine",
    )(logits)


def sum_kernel(parts_ref, out_ref):
    top = lax.broadcasted_iota(jnp.int32, (2, 8, HALF), 1) < 4
    for i in range(4):
        part = parts_ref[16 * i : 16 * i + 16].astype(F32).reshape(4, 4, 8, HALF)
        part = jnp.sum(part, axis=1).reshape(2, 2, 8, HALF)
        even, odd = part[:, 0], part[:, 1]
        first = jnp.where(top, even, pltpu.roll(odd, 4, 1))
        second = jnp.where(top, pltpu.roll(even, 4, 1), odd)
        rows = pl.ds(16 * i, 16)
        out_ref[0, rows] = first.reshape(16, HALF).astype(BF16)
        out_ref[1, rows] = second.reshape(16, HALF).astype(BF16)


def sum_parts(parts):
    return pl.pallas_call(
        sum_kernel,
        out_shape=jax.ShapeDtypeStruct((2, 64, HALF), BF16),
        compiler_params=pltpu.CompilerParams(vmem_limit_bytes=24 << 20),
        name="sum_parts",
    )(parts)


def mix_kernel(combine_ref, own_ref, oth_ref, out_ref):
    core = lax.axis_index("core")
    mine = pl.ds(pl.multiple_of(core * HALF, 128), HALF)
    other = pl.ds(pl.multiple_of((1 - core) * HALF, 128), HALF)
    weights = combine_ref[0]
    out_ref[0, :, mine] = jnp.dot(weights, own_ref[0], preferred_element_type=F32).astype(BF16)
    out_ref[0, :, other] = jnp.dot(weights, oth_ref[0], preferred_element_type=F32).astype(BF16)


def mix(weights, own, oth):
    clips, count, slots = weights.shape
    rows = 512
    width = 2 * HALF
    return pl.pallas_call(
        mix_kernel,
        out_shape=jax.ShapeDtypeStruct((clips, count, width), BF16),
        grid=(clips, count // rows),
        in_specs=[
            pl.BlockSpec((1, rows, slots), lambda b, i: (b, i, 0)),
            pl.BlockSpec((1, slots, HALF), lambda b, i: (b, 0, 0)),
            pl.BlockSpec((1, slots, HALF), lambda b, i: (b, 0, 0)),
        ],
        out_specs=pl.BlockSpec((1, rows, width), lambda b, i: (b, i, 0)),
        compiler_params=pltpu.CompilerParams(vmem_limit_bytes=32 << 20),
        name="mix",
    )(weights, own, oth)


def swap(x):
    return lax.ppermute(x, "core", [(0, 1), (1, 0)])


def exchange(x):
    return lax.all_to_all(x, ("dp", "x"), 0, 0, tiled=True)


def on_device(tokens, slot_param, w_in, w_out):
    send, keep, logits = gather(
        pltpu.with_memory_space_constraint(tokens, pltpu.HBM),
        pltpu.with_memory_space_constraint(slot_param.T, pltpu.HBM),
    )
    own = reduce(exchange(pack(keep, swap(send))))
    weights = combine(logits)
    send, keep = expert(own, swap(own), w_in, w_out)
    summed = (keep + swap(send).astype(F32)).astype(BF16).reshape(16, 1, 8, HALF)
    own = sum_parts(exchange(jnp.broadcast_to(summed, (16, 4, 8, HALF)).reshape(64, 8, HALF)))
    return mix(weights, own, swap(own))


def solution(mesh):
    ctx = ("x", "core")
    split = jax.sharding.Mesh(np.asarray(mesh.devices).reshape(16, 4, 2), ("dp",) + ctx)
    placed = (P("dp", ctx, None), P(), P("dp", None, ctx), P("dp", ctx, None))
    return jax.shard_map(
        on_device, mesh=split, in_specs=placed, out_specs=P("dp", ctx, None), check_vma=False
    )
```

```python
import functools

import jax
import jax.numpy as jnp
import numpy as np
from jax import lax
from jax.experimental import pallas as pl
from jax.experimental.pallas import tpu as pltpu
from jax.sharding import PartitionSpec as P

F32 = jnp.float32
BF16 = jnp.bfloat16
HALF = 640
WIDE = HALF + 128
NT = (((1,), (1,)), ((), ()))


def columns(half):
    core = lax.axis_index("core")
    return pl.ds(pl.multiple_of((core if half == 0 else 1 - core) * HALF, 128), HALF)


def stats_block(peak, total):
    high = total.astype(BF16).astype(F32)
    lane = lax.broadcasted_iota(jnp.int32, (peak.shape[0], 128), 1)
    return jnp.where(lane == 0, peak, jnp.where(lane == 1, high, jnp.where(lane == 2, total - high, 0.0)))


def gather_kernel(
    pieces, tokens_hbm, slots_hbm, send_ref, stats_ref, dispatch_ref, logits_ref, tokens_ref, slots, sems
):
    clips, count, _ = tokens_ref.shape
    step = count // pieces

    def copy(b, i):
        rows = pl.ds(i * step, step)
        return pltpu.make_async_copy(tokens_hbm.at[b, rows], tokens_ref.at[b, rows], sems.at[b, i])

    slots_copy = pltpu.make_async_copy(slots_hbm, slots, sems.at[clips, 0])
    slots_copy.start()
    for b in range(clips):
        for i in range(pieces):
            copy(b, i).start()
    slots_copy.wait()
    for b in range(clips):
        for i in range(pieces):
            copy(b, i).wait()
            rows = pl.ds(i * step, step)
            logits_ref[b, :, rows] = lax.dot_general(
                slots[...], tokens_ref[b, rows, :], NT, preferred_element_type=F32
            )
    for b in range(clips):
        logits = logits_ref[b]
        peak = jnp.max(logits, axis=1, keepdims=True).astype(BF16).astype(F32)
        expd = jnp.exp(logits - peak)
        stats = stats_block(peak, jnp.sum(expd, axis=1, keepdims=True))
        dispatch_ref[b] = expd.astype(BF16)
        stats_ref[b] = stats
        send_ref[b, :, pl.ds(HALF, 128)] = stats.astype(BF16)
        send_ref[b, :, pl.ds(0, HALF)] = jnp.dot(
            dispatch_ref[b], tokens_ref[b, :, columns(1)], preferred_element_type=F32
        ).astype(BF16)


def gather(tokens, slots_t):
    clips, count, width = tokens.shape
    slots = slots_t.shape[0]
    pieces = 2
    vmem = pl.BlockSpec(memory_space=pltpu.VMEM)
    return pl.pallas_call(
        functools.partial(gather_kernel, pieces),
        out_shape=[
            pltpu.VMEM((clips, slots, WIDE), BF16),
            pltpu.VMEM((clips, slots, 128), F32),
            pltpu.VMEM((clips, slots, count), BF16),
            pltpu.VMEM((clips, slots, count), F32),
            pltpu.VMEM((clips, count, width), BF16),
        ],
        in_specs=[pl.BlockSpec(memory_space=pl.ANY)] * 2,
        out_specs=[vmem] * 5,
        scratch_shapes=[pltpu.VMEM((slots, width), BF16), pltpu.SemaphoreType.DMA((clips + 1, pieces))],
        compiler_params=pltpu.CompilerParams(vmem_limit_bytes=56 << 20),
        cost_estimate=pl.CostEstimate(
            flops=3 * clips * slots * count * width,
            bytes_accessed=2 * clips * count * width,
            transcendentals=clips * slots * count,
        ),
        name="gather",
    )(tokens, slots_t)


def keep_kernel(dispatch_ref, tokens_ref, out_ref):
    for b in range(dispatch_ref.shape[0]):
        out_ref[b] = jnp.dot(dispatch_ref[b], tokens_ref[b, :, columns(0)], preferred_element_type=F32)


def keep_half(dispatch, tokens):
    clips, slots, count = dispatch.shape
    return pl.pallas_call(
        keep_kernel,
        out_shape=pltpu.VMEM((clips, slots, HALF), F32),
        compiler_params=pltpu.CompilerParams(vmem_limit_bytes=16 << 20),
        cost_estimate=pl.CostEstimate(
            flops=2 * clips * slots * count * HALF, bytes_accessed=2 * tokens.size, transcendentals=0
        ),
        name="keep_half",
    )(dispatch, tokens)


def pack_kernel(keep_ref, stats_ref, recv_ref, out_ref):
    halves = []
    for b in range(2):
        kept, stats, got = keep_ref[b], stats_ref[b], recv_ref[b].astype(F32)
        peak_k, peak_g = stats[:, :1], got[:, HALF : HALF + 1]
        peak = jnp.maximum(peak_k, peak_g)
        scale_k, scale_g = jnp.exp(peak_k - peak), jnp.exp(peak_g - peak)
        total = scale_k * (stats[:, 1:2] + stats[:, 2:3]) + scale_g * (
            got[:, HALF + 1 : HALF + 2] + got[:, HALF + 2 : HALF + 3]
        )
        value = scale_k * kept + scale_g * got[:, :HALF]
        halves.append(jnp.concatenate([value, stats_block(peak, total)], axis=1).reshape(8, 8, WIDE))
    first, second = halves
    top = lax.broadcasted_iota(jnp.int32, first.shape, 1) < 4
    even = jnp.where(top, first, pltpu.roll(second, 4, 1)).astype(BF16)
    odd = jnp.where(top, pltpu.roll(first, 4, 1), second).astype(BF16)
    for j in range(8):
        for x in range(4):
            out_ref[8 * j + x] = even[j]
            out_ref[8 * j + 4 + x] = odd[j]


def pack(keep, stats, recv):
    return pl.pallas_call(
        pack_kernel,
        out_shape=jax.ShapeDtypeStruct((64, 8, WIDE), BF16),
        compiler_params=pltpu.CompilerParams(vmem_limit_bytes=24 << 20),
        cost_estimate=pl.CostEstimate(flops=1 << 36, bytes_accessed=100 << 20, transcendentals=0),
        name="pack",
    )(keep, stats, recv)


def reduce_kernel(parts_ref, out_ref):
    for i in range(8):
        part = parts_ref[8 * i : 8 * i + 8].astype(F32).reshape(2, 4, 8, WIDE)
        peak = part[..., HALF : HALF + 1]
        weight = jnp.exp(peak - jnp.max(peak, axis=1, keepdims=True))
        total = weight * (part[..., HALF + 1 : HALF + 2] + part[..., HALF + 2 : HALF + 3])
        weight = weight / jnp.sum(total, axis=1, keepdims=True)
        slot_in = jnp.sum(weight * part[..., :HALF], axis=1)
        out_ref[pl.ds(16 * i, 16), :] = slot_in.reshape(16, HALF).astype(BF16)


def reduce(parts):
    return pl.pallas_call(
        reduce_kernel,
        out_shape=jax.ShapeDtypeStruct((128, HALF), BF16),
        compiler_params=pltpu.CompilerParams(vmem_limit_bytes=24 << 20),
        name="reduce",
    )(parts)


def own_expert(rows, weights, lanes):
    experts = weights.shape[0]
    slot = lax.broadcasted_iota(jnp.int32, (rows.shape[0], 1), 0) % experts
    out = None
    for e in range(experts):
        here = jnp.dot(rows, weights[(e, *lanes)], preferred_element_type=F32)
        out = here if e == 0 else jnp.where(slot == e, here, out)
    return out


def first_kernel(own_ref, w_in, pre_ref):
    pre_ref[...] = own_expert(own_ref[...], w_in, (columns(0), slice(None)))


def second_kernel(pre_ref, oth_ref, w_in, w_out, hidden_ref, send_ref):
    value = pre_ref[...] + own_expert(oth_ref[...], w_in, (columns(1), slice(None)))
    hidden_ref[...] = (0.5 * value * (1.0 + lax.erf(value * np.float32(np.sqrt(0.5))))).astype(BF16)
    send_ref[...] = own_expert(hidden_ref[...], w_out, (slice(None), columns(1))).astype(BF16)


def third_kernel(hidden_ref, w_out, keep_ref):
    keep_ref[...] = own_expert(hidden_ref[...], w_out, (slice(None), columns(0)))


def stage(kernel, name, outs, *operands):
    return pl.pallas_call(
        kernel,
        out_shape=outs,
        compiler_params=pltpu.CompilerParams(vmem_limit_bytes=24 << 20),
        cost_estimate=pl.CostEstimate(
            flops=128 * sum(x.size for x in operands), bytes_accessed=2 * sum(x.size for x in operands), transcendentals=0
        ),
        name=name,
    )(*operands)


def combine_kernel(logits_ref, out_ref):
    for b in range(2):
        logits = logits_ref[b]
        expd = jnp.exp(logits - jnp.max(logits, axis=0, keepdims=True))
        combine = expd / jnp.sum(expd, axis=0, keepdims=True)
        out_ref[b] = combine.T.astype(BF16)


def combine(logits):
    clips, slots, count = logits.shape
    return pl.pallas_call(
        combine_kernel,
        out_shape=jax.ShapeDtypeStruct((clips, count, slots), BF16),
        compiler_params=pltpu.CompilerParams(vmem_limit_bytes=24 << 20),
        cost_estimate=pl.CostEstimate(flops=8 * logits.size, bytes_accessed=6 * logits.size, transcendentals=logits.size),
        name="combine",
    )(logits)


def sum_kernel(parts_ref, out_ref):
    top = lax.broadcasted_iota(jnp.int32, (2, 8, HALF), 1) < 4
    for i in range(4):
        part = parts_ref[16 * i : 16 * i + 16].astype(F32).reshape(4, 4, 8, HALF)
        part = jnp.sum(part, axis=1).reshape(2, 2, 8, HALF)
        even, odd = part[:, 0], part[:, 1]
        first = jnp.where(top, even, pltpu.roll(odd, 4, 1))
        second = jnp.where(top, pltpu.roll(even, 4, 1), odd)
        rows = pl.ds(16 * i, 16)
        out_ref[0, rows] = first.reshape(16, HALF).astype(BF16)
        out_ref[1, rows] = second.reshape(16, HALF).astype(BF16)


def sum_parts(parts):
    return pl.pallas_call(
        sum_kernel,
        out_shape=jax.ShapeDtypeStruct((2, 64, HALF), BF16),
        compiler_params=pltpu.CompilerParams(vmem_limit_bytes=24 << 20),
        name="sum_parts",
    )(parts)


def mix_own_kernel(combine_ref, own_ref, out_ref):
    for b in range(combine_ref.shape[0]):
        out_ref[b] = jnp.dot(combine_ref[b], own_ref[b], preferred_element_type=F32).astype(BF16)


def mix_kernel(pieces, combine_ref, mixed_ref, oth_ref, out_hbm, mixed, sems):
    clips, count, _ = mixed.shape
    copies = [
        pltpu.make_async_copy(mixed_ref.at[b], out_hbm.at[b, :, columns(0)], sems.at[clips, b]) for b in range(clips)
    ]
    for copy in copies:
        copy.start()
    for b in range(clips):
        for i in range(pieces):
            rows = pl.ds(i * (count // pieces), count // pieces)
            mixed[b, rows] = jnp.dot(combine_ref[b, rows], oth_ref[b], preferred_element_type=F32).astype(BF16)
            copies.append(pltpu.make_async_copy(mixed.at[b, rows], out_hbm.at[b, rows, columns(1)], sems.at[b, i]))
            copies[-1].start()
    for copy in copies:
        copy.wait()


def mix(weights, mixed, oth):
    clips, count, _ = weights.shape
    pieces = 2
    return pl.pallas_call(
        functools.partial(mix_kernel, pieces),
        out_shape=jax.ShapeDtypeStruct((clips, count, 2 * HALF), BF16),
        in_specs=[pl.BlockSpec(memory_space=pltpu.VMEM)] * 3,
        out_specs=pl.BlockSpec(memory_space=pl.ANY),
        scratch_shapes=[pltpu.VMEM((clips, count, HALF), BF16), pltpu.SemaphoreType.DMA((clips + 1, pieces))],
        compiler_params=pltpu.CompilerParams(vmem_limit_bytes=32 << 20),
        name="mix",
    )(weights, mixed, oth)


def swap(x):
    return lax.ppermute(x, "core", [(0, 1), (1, 0)])


def exchange(x):
    return lax.all_to_all(x, ("dp", "x"), 0, 0, tiled=True)


def on_device(tokens, slot_param, w_in, w_out):
    send, stats, dispatch, logits, held = gather(
        pltpu.with_memory_space_constraint(tokens, pltpu.HBM),
        pltpu.with_memory_space_constraint(slot_param.T, pltpu.HBM),
    )
    keep, weights = lax.optimization_barrier((keep_half(dispatch, held), combine(logits)))
    own = reduce(exchange(pack(keep, stats, swap(send))))
    pre = stage(first_kernel, "first", pltpu.VMEM((128, HALF), F32), own, w_in)
    outs = [pltpu.VMEM((128, HALF), BF16)] * 2
    hidden, send = stage(second_kernel, "second", outs, pre, swap(own), w_in, w_out)
    keep = stage(third_kernel, "third", pltpu.VMEM((128, HALF), F32), hidden, w_out)
    summed = (keep + swap(send).astype(F32)).astype(BF16).reshape(16, 1, 8, HALF)
    own = sum_parts(exchange(jnp.broadcast_to(summed, (16, 4, 8, HALF)).reshape(64, 8, HALF)))
    mixed = stage(mix_own_kernel, "mix_own", pltpu.VMEM(weights.shape[:2] + (HALF,), BF16), weights, own)
    return mix(weights, mixed, swap(own))


def solution(mesh):
    ctx = ("x", "core")
    split = jax.sharding.Mesh(np.asarray(mesh.devices).reshape(16, 4, 2), ("dp",) + ctx)
    placed = (P("dp", ctx, None), P(), P("dp", None, ctx), P("dp", ctx, None))
    return jax.shard_map(
        on_device, mesh=split, in_specs=placed, out_specs=P("dp", ctx, None), check_vma=False
    )
```

```python
import functools

import jax
import jax.numpy as jnp
import numpy as np
from jax import lax
from jax.experimental import pallas as pl
from jax.experimental.pallas import tpu as pltpu
from jax.sharding import PartitionSpec as P

F32 = jnp.float32
BF16 = jnp.bfloat16
HALF = 640
WIDE = HALF + 128
NT = (((1,), (1,)), ((), ()))


def columns(half):
    core = lax.axis_index("core")
    return pl.ds(pl.multiple_of((core if half == 0 else 1 - core) * HALF, 128), HALF)


def stats_block(peak, total):
    high = total.astype(BF16).astype(F32)
    lane = lax.broadcasted_iota(jnp.int32, (peak.shape[0], 128), 1)
    return jnp.where(lane == 0, peak, jnp.where(lane == 1, high, jnp.where(lane == 2, total - high, 0.0)))


def gather_kernel(
    pieces, tokens_hbm, slots_hbm, send_ref, stats_ref, dispatch_ref, logits_ref, tokens_ref, slots, sems
):
    clips, count, _ = tokens_ref.shape
    step = count // pieces

    def copy(b, i):
        rows = pl.ds(i * step, step)
        return pltpu.make_async_copy(tokens_hbm.at[b, rows], tokens_ref.at[b, rows], sems.at[b, i])

    slots_copy = pltpu.make_async_copy(slots_hbm, slots, sems.at[clips, 0])
    slots_copy.start()
    for b in range(clips):
        for i in range(pieces):
            copy(b, i).start()
    slots_copy.wait()
    for b in range(clips):
        for i in range(pieces):
            copy(b, i).wait()
            rows = pl.ds(i * step, step)
            logits_ref[b, :, rows] = lax.dot_general(
                slots[...], tokens_ref[b, rows, :], NT, preferred_element_type=F32
            )
    for b in range(clips):
        logits = logits_ref[b]
        peak = jnp.max(logits, axis=1, keepdims=True).astype(BF16).astype(F32)
        expd = jnp.exp(logits - peak)
        stats = stats_block(peak, jnp.sum(expd, axis=1, keepdims=True))
        dispatch_ref[b] = expd.astype(BF16)
        stats_ref[b] = stats
        send_ref[b, :, pl.ds(HALF, 128)] = stats.astype(BF16)
        send_ref[b, :, pl.ds(0, HALF)] = jnp.dot(
            dispatch_ref[b], tokens_ref[b, :, columns(1)], preferred_element_type=F32
        ).astype(BF16)


def gather(tokens, slots_t):
    clips, count, width = tokens.shape
    slots = slots_t.shape[0]
    pieces = 2
    vmem = pl.BlockSpec(memory_space=pltpu.VMEM)
    return pl.pallas_call(
        functools.partial(gather_kernel, pieces),
        out_shape=[
            pltpu.VMEM((clips, slots, WIDE), BF16),
            pltpu.VMEM((clips, slots, 128), F32),
            pltpu.VMEM((clips, slots, count), BF16),
            pltpu.VMEM((clips, slots, count), F32),
            pltpu.VMEM((clips, count, width), BF16),
        ],
        in_specs=[pl.BlockSpec(memory_space=pl.ANY)] * 2,
        out_specs=[vmem] * 5,
        scratch_shapes=[pltpu.VMEM((slots, width), BF16), pltpu.SemaphoreType.DMA((clips + 1, pieces))],
        compiler_params=pltpu.CompilerParams(vmem_limit_bytes=56 << 20),
        cost_estimate=pl.CostEstimate(
            flops=3 * clips * slots * count * width,
            bytes_accessed=2 * clips * count * width,
            transcendentals=clips * slots * count,
        ),
        name="gather",
    )(tokens, slots_t)


def keep_kernel(dispatch_ref, tokens_ref, out_ref):
    for b in range(dispatch_ref.shape[0]):
        out_ref[b] = jnp.dot(dispatch_ref[b], tokens_ref[b, :, columns(0)], preferred_element_type=F32)


def keep_half(dispatch, tokens):
    clips, slots, count = dispatch.shape
    return pl.pallas_call(
        keep_kernel,
        out_shape=pltpu.VMEM((clips, slots, HALF), F32),
        compiler_params=pltpu.CompilerParams(vmem_limit_bytes=16 << 20),
        cost_estimate=pl.CostEstimate(
            flops=2 * clips * slots * count * HALF, bytes_accessed=2 * tokens.size, transcendentals=0
        ),
        name="keep_half",
    )(dispatch, tokens)


def pack_kernel(keep_ref, stats_ref, recv_ref, out_ref):
    halves = []
    for b in range(2):
        kept, stats, got = keep_ref[b], stats_ref[b], recv_ref[b].astype(F32)
        peak_k, peak_g = stats[:, :1], got[:, HALF : HALF + 1]
        peak = jnp.maximum(peak_k, peak_g)
        scale_k, scale_g = jnp.exp(peak_k - peak), jnp.exp(peak_g - peak)
        total = scale_k * (stats[:, 1:2] + stats[:, 2:3]) + scale_g * (
            got[:, HALF + 1 : HALF + 2] + got[:, HALF + 2 : HALF + 3]
        )
        value = scale_k * kept + scale_g * got[:, :HALF]
        halves.append(jnp.concatenate([value, stats_block(peak, total)], axis=1).reshape(8, 8, WIDE))
    first, second = halves
    top = lax.broadcasted_iota(jnp.int32, first.shape, 1) < 4
    even = jnp.where(top, first, pltpu.roll(second, 4, 1)).astype(BF16)
    odd = jnp.where(top, pltpu.roll(first, 4, 1), second).astype(BF16)
    for j in range(8):
        for x in range(4):
            out_ref[8 * j + x] = even[j]
            out_ref[8 * j + 4 + x] = odd[j]


def pack(keep, stats, recv):
    return pl.pallas_call(
        pack_kernel,
        out_shape=jax.ShapeDtypeStruct((64, 8, WIDE), BF16),
        compiler_params=pltpu.CompilerParams(vmem_limit_bytes=24 << 20),
        cost_estimate=pl.CostEstimate(flops=1 << 36, bytes_accessed=100 << 20, transcendentals=0),
        name="pack",
    )(keep, stats, recv)


def reduce_kernel(parts_ref, out_ref):
    stats = parts_ref[:, :, pl.ds(HALF, 128)].astype(F32).reshape(16, 4, 8, 128)
    peak = stats[..., :1]
    weight = jnp.exp(peak - jnp.max(peak, axis=1, keepdims=True))
    total = jnp.sum(weight * (stats[..., 1:2] + stats[..., 2:3]), axis=1, keepdims=True)
    weight = jnp.broadcast_to(weight / total, (16, 4, 8, 128))
    for i in range(8):
        scale = jnp.concatenate([weight[2 * i : 2 * i + 2]] * (HALF // 128), axis=-1)
        part = parts_ref[8 * i : 8 * i + 8, :, pl.ds(0, HALF)].astype(F32).reshape(2, 4, 8, HALF)
        out_ref[pl.ds(16 * i, 16), :] = jnp.sum(scale * part, axis=1).reshape(16, HALF).astype(BF16)


def reduce(parts):
    return pl.pallas_call(
        reduce_kernel,
        out_shape=jax.ShapeDtypeStruct((128, HALF), BF16),
        compiler_params=pltpu.CompilerParams(vmem_limit_bytes=24 << 20),
        name="reduce",
    )(parts)


def own_expert(rows, weights, lanes):
    experts = weights.shape[0]
    slot = lax.broadcasted_iota(jnp.int32, (rows.shape[0], 1), 0) % experts
    out = None
    for e in range(0, experts, 2):
        pair = jnp.concatenate([weights[(e, *lanes)], weights[(e + 1, *lanes)]], axis=1)
        here = jnp.dot(rows, pair, preferred_element_type=F32)
        here = jnp.where(slot % 2 == 0, here[:, :HALF], here[:, HALF:])
        out = here if e == 0 else jnp.where(slot >= e, here, out)
    return out


def first_kernel(own_ref, w_in, pre_ref):
    pre_ref[...] = own_expert(own_ref[...], w_in, (columns(0), slice(None)))


def second_kernel(pre_ref, oth_ref, w_in, w_out, hidden_ref, send_ref):
    value = pre_ref[...] + own_expert(oth_ref[...], w_in, (columns(1), slice(None)))
    hidden_ref[...] = (0.5 * value * (1.0 + lax.erf(value * np.float32(np.sqrt(0.5))))).astype(BF16)
    send_ref[...] = own_expert(hidden_ref[...], w_out, (slice(None), columns(1))).astype(BF16)


def third_kernel(hidden_ref, w_out, keep_ref):
    keep_ref[...] = own_expert(hidden_ref[...], w_out, (slice(None), columns(0)))


def stage(kernel, name, outs, *operands):
    return pl.pallas_call(
        kernel,
        out_shape=outs,
        compiler_params=pltpu.CompilerParams(vmem_limit_bytes=24 << 20),
        cost_estimate=pl.CostEstimate(
            flops=128 * sum(x.size for x in operands), bytes_accessed=2 * sum(x.size for x in operands), transcendentals=0
        ),
        name=name,
    )(*operands)


def combine_kernel(logits_ref, out_ref):
    for b in range(2):
        logits = logits_ref[b]
        expd = jnp.exp(logits - jnp.max(logits, axis=0, keepdims=True))
        combine = expd / jnp.sum(expd, axis=0, keepdims=True)
        out_ref[b] = combine.T.astype(BF16)


def combine(logits):
    clips, slots, count = logits.shape
    return pl.pallas_call(
        combine_kernel,
        out_shape=jax.ShapeDtypeStruct((clips, count, slots), BF16),
        compiler_params=pltpu.CompilerParams(vmem_limit_bytes=24 << 20),
        cost_estimate=pl.CostEstimate(flops=8 * logits.size, bytes_accessed=6 * logits.size, transcendentals=logits.size),
        name="combine",
    )(logits)


def sum_kernel(parts_ref, out_ref):
    top = lax.broadcasted_iota(jnp.int32, (2, 8, HALF), 1) < 4
    for i in range(4):
        part = parts_ref[16 * i : 16 * i + 16].astype(F32).reshape(4, 4, 8, HALF)
        part = jnp.sum(part, axis=1).reshape(2, 2, 8, HALF)
        even, odd = part[:, 0], part[:, 1]
        first = jnp.where(top, even, pltpu.roll(odd, 4, 1))
        second = jnp.where(top, pltpu.roll(even, 4, 1), odd)
        rows = pl.ds(16 * i, 16)
        out_ref[0, rows] = first.reshape(16, HALF).astype(BF16)
        out_ref[1, rows] = second.reshape(16, HALF).astype(BF16)


def sum_parts(parts):
    return pl.pallas_call(
        sum_kernel,
        out_shape=jax.ShapeDtypeStruct((2, 64, HALF), BF16),
        compiler_params=pltpu.CompilerParams(vmem_limit_bytes=24 << 20),
        name="sum_parts",
    )(parts)


def mix_own_kernel(combine_ref, own_ref, out_ref):
    for b in range(combine_ref.shape[0]):
        out_ref[b] = jnp.dot(combine_ref[b], own_ref[b], preferred_element_type=F32).astype(BF16)


def mix_kernel(pieces, combine_ref, mixed_ref, oth_ref, out_hbm, mixed, sems):
    clips, count, _ = mixed.shape
    copies = [
        pltpu.make_async_copy(mixed_ref.at[b], out_hbm.at[b, :, columns(0)], sems.at[clips, b]) for b in range(clips)
    ]
    for copy in copies:
        copy.start()
    for b in range(clips):
        for i in range(pieces):
            rows = pl.ds(i * (count // pieces), count // pieces)
            mixed[b, rows] = jnp.dot(combine_ref[b, rows], oth_ref[b], preferred_element_type=F32).astype(BF16)
            copies.append(pltpu.make_async_copy(mixed.at[b, rows], out_hbm.at[b, rows, columns(1)], sems.at[b, i]))
            copies[-1].start()
    for copy in copies:
        copy.wait()


def mix(weights, mixed, oth):
    clips, count, _ = weights.shape
    pieces = 2
    return pl.pallas_call(
        functools.partial(mix_kernel, pieces),
        out_shape=jax.ShapeDtypeStruct((clips, count, 2 * HALF), BF16),
        in_specs=[pl.BlockSpec(memory_space=pltpu.VMEM)] * 3,
        out_specs=pl.BlockSpec(memory_space=pl.ANY),
        scratch_shapes=[pltpu.VMEM((clips, count, HALF), BF16), pltpu.SemaphoreType.DMA((clips + 1, pieces))],
        compiler_params=pltpu.CompilerParams(vmem_limit_bytes=32 << 20),
        name="mix",
    )(weights, mixed, oth)


def swap(x):
    return lax.ppermute(x, "core", [(0, 1), (1, 0)])


def exchange(x):
    return lax.all_to_all(x, ("dp", "x"), 0, 0, tiled=True)


def on_device(tokens, slot_param, w_in, w_out):
    send, stats, dispatch, logits, held = gather(
        pltpu.with_memory_space_constraint(tokens, pltpu.HBM),
        pltpu.with_memory_space_constraint(slot_param.T, pltpu.HBM),
    )
    keep, weights = lax.optimization_barrier((keep_half(dispatch, held), combine(logits)))
    own = reduce(exchange(pack(keep, stats, swap(send))))
    pre = stage(first_kernel, "first", pltpu.VMEM((128, HALF), F32), own, w_in)
    outs = [pltpu.VMEM((128, HALF), BF16)] * 2
    hidden, send = stage(second_kernel, "second", outs, pre, swap(own), w_in, w_out)
    keep = stage(third_kernel, "third", pltpu.VMEM((128, HALF), F32), hidden, w_out)
    summed = (keep + swap(send).astype(F32)).astype(BF16).reshape(16, 1, 8, HALF)
    own = sum_parts(exchange(jnp.broadcast_to(summed, (16, 4, 8, HALF)).reshape(64, 8, HALF)))
    mixed = stage(mix_own_kernel, "mix_own", pltpu.VMEM(weights.shape[:2] + (HALF,), BF16), weights, own)
    return mix(weights, mixed, swap(own))


def solution(mesh):
    ctx = ("x", "core")
    split = jax.sharding.Mesh(np.asarray(mesh.devices).reshape(16, 4, 2), ("dp",) + ctx)
    placed = (P("dp", ctx, None), P(), P("dp", None, ctx), P("dp", ctx, None))
    return jax.shard_map(
        on_device, mesh=split, in_specs=placed, out_specs=P("dp", ctx, None), check_vma=False
    )
```

```python
import functools

import jax
import jax.numpy as jnp
import numpy as np
from jax import lax
from jax.experimental import pallas as pl
from jax.experimental.pallas import tpu as pltpu
from jax.sharding import PartitionSpec as P

F32 = jnp.float32
BF16 = jnp.bfloat16
HALF = 640
WIDE = HALF + 128
EARLY = 256
NT = (((1,), (1,)), ((), ()))


def columns(half):
    core = lax.axis_index("core")
    return pl.ds(pl.multiple_of((core if half == 0 else 1 - core) * HALF, 128), HALF)


def stats_block(peak, total):
    high = total.astype(BF16).astype(F32)
    lane = lax.broadcasted_iota(jnp.int32, (peak.shape[0], 128), 1)
    return jnp.where(lane == 0, peak, jnp.where(lane == 1, high, jnp.where(lane == 2, total - high, 0.0)))


def gather_kernel(
    pieces, tokens_hbm, slots_hbm, send_ref, stats_ref, dispatch_ref, logits_ref, tokens_ref, slots, sems
):
    clips, count, _ = tokens_ref.shape
    step = count // pieces

    def copy(b, i):
        rows = pl.ds(i * step, step)
        return pltpu.make_async_copy(tokens_hbm.at[b, rows], tokens_ref.at[b, rows], sems.at[b, i])

    slots_copy = pltpu.make_async_copy(slots_hbm, slots, sems.at[clips, 0])
    slots_copy.start()
    for b in range(clips):
        for i in range(pieces):
            copy(b, i).start()
    slots_copy.wait()
    for b in range(clips):
        for i in range(pieces):
            copy(b, i).wait()
            rows = pl.ds(i * step, step)
            logits_ref[b, :, rows] = lax.dot_general(
                slots[...], tokens_ref[b, rows, :], NT, preferred_element_type=F32
            )
    for b in range(clips):
        logits = logits_ref[b]
        peak = jnp.max(logits, axis=1, keepdims=True).astype(BF16).astype(F32)
        expd = jnp.exp(logits - peak)
        stats = stats_block(peak, jnp.sum(expd, axis=1, keepdims=True))
        dispatch_ref[b] = expd.astype(BF16)
        stats_ref[b] = stats
        send_ref[b, :, pl.ds(HALF, 128)] = stats.astype(BF16)
        send_ref[b, :, pl.ds(0, HALF)] = jnp.dot(
            dispatch_ref[b], tokens_ref[b, :, columns(1)], preferred_element_type=F32
        ).astype(BF16)


def gather(tokens, slots_t):
    clips, count, width = tokens.shape
    slots = slots_t.shape[0]
    pieces = 2
    vmem = pl.BlockSpec(memory_space=pltpu.VMEM)
    return pl.pallas_call(
        functools.partial(gather_kernel, pieces),
        out_shape=[
            pltpu.VMEM((clips, slots, WIDE), BF16),
            pltpu.VMEM((clips, slots, 128), F32),
            pltpu.VMEM((clips, slots, count), BF16),
            pltpu.VMEM((clips, slots, count), F32),
            pltpu.VMEM((clips, count, width), BF16),
        ],
        in_specs=[pl.BlockSpec(memory_space=pl.ANY)] * 2,
        out_specs=[vmem] * 5,
        scratch_shapes=[pltpu.VMEM((slots, width), BF16), pltpu.SemaphoreType.DMA((clips + 1, pieces))],
        compiler_params=pltpu.CompilerParams(vmem_limit_bytes=56 << 20),
        cost_estimate=pl.CostEstimate(
            flops=3 * clips * slots * count * width,
            bytes_accessed=2 * clips * count * width,
            transcendentals=clips * slots * count,
        ),
        name="gather",
    )(tokens, slots_t)


def keep_kernel(dispatch_ref, tokens_ref, out_ref):
    for b in range(dispatch_ref.shape[0]):
        out_ref[b] = jnp.dot(dispatch_ref[b], tokens_ref[b, :, columns(0)], preferred_element_type=F32)


def keep_half(dispatch, tokens):
    clips, slots, count = dispatch.shape
    return pl.pallas_call(
        keep_kernel,
        out_shape=pltpu.VMEM((clips, slots, HALF), F32),
        compiler_params=pltpu.CompilerParams(vmem_limit_bytes=16 << 20),
        cost_estimate=pl.CostEstimate(
            flops=2 * clips * slots * count * HALF, bytes_accessed=2 * tokens.size, transcendentals=0
        ),
        name="keep_half",
    )(dispatch, tokens)


def pack_kernel(keep_ref, stats_ref, recv_ref, out_ref):
    halves = []
    for b in range(2):
        kept, stats, got = keep_ref[b], stats_ref[b], recv_ref[b].astype(F32)
        peak_k, peak_g = stats[:, :1], got[:, HALF : HALF + 1]
        peak = jnp.maximum(peak_k, peak_g)
        scale_k, scale_g = jnp.exp(peak_k - peak), jnp.exp(peak_g - peak)
        total = scale_k * (stats[:, 1:2] + stats[:, 2:3]) + scale_g * (
            got[:, HALF + 1 : HALF + 2] + got[:, HALF + 2 : HALF + 3]
        )
        value = scale_k * kept + scale_g * got[:, :HALF]
        halves.append(jnp.concatenate([value, stats_block(peak, total)], axis=1).reshape(8, 8, WIDE))
    first, second = halves
    top = lax.broadcasted_iota(jnp.int32, first.shape, 1) < 4
    even = jnp.where(top, first, pltpu.roll(second, 4, 1)).astype(BF16)
    odd = jnp.where(top, pltpu.roll(first, 4, 1), second).astype(BF16)
    for j in range(8):
        for x in range(4):
            out_ref[8 * j + x] = even[j]
            out_ref[8 * j + 4 + x] = odd[j]


def pack(keep, stats, recv):
    return pl.pallas_call(
        pack_kernel,
        out_shape=jax.ShapeDtypeStruct((64, 8, WIDE), BF16),
        compiler_params=pltpu.CompilerParams(vmem_limit_bytes=24 << 20),
        cost_estimate=pl.CostEstimate(flops=1 << 36, bytes_accessed=100 << 20, transcendentals=0),
        name="pack",
    )(keep, stats, recv)


def reduce_kernel(parts_ref, out_ref):
    stats = parts_ref[:, :, pl.ds(HALF, 128)].astype(F32).reshape(16, 4, 8, 128)
    peak = stats[..., :1]
    weight = jnp.exp(peak - jnp.max(peak, axis=1, keepdims=True))
    total = jnp.sum(weight * (stats[..., 1:2] + stats[..., 2:3]), axis=1, keepdims=True)
    weight = jnp.broadcast_to(weight / total, (16, 4, 8, 128))
    for i in range(8):
        scale = jnp.concatenate([weight[2 * i : 2 * i + 2]] * (HALF // 128), axis=-1)
        part = parts_ref[8 * i : 8 * i + 8, :, pl.ds(0, HALF)].astype(F32).reshape(2, 4, 8, HALF)
        out_ref[pl.ds(16 * i, 16), :] = jnp.sum(scale * part, axis=1).reshape(16, HALF).astype(BF16)


def reduce(parts):
    return pl.pallas_call(
        reduce_kernel,
        out_shape=jax.ShapeDtypeStruct((128, HALF), BF16),
        compiler_params=pltpu.CompilerParams(vmem_limit_bytes=24 << 20),
        name="reduce",
    )(parts)


def own_expert(rows, weights, lanes):
    experts = weights.shape[0]
    slot = lax.broadcasted_iota(jnp.int32, (rows.shape[0], 1), 0) % experts
    out = None
    for e in range(0, experts, 2):
        pair = jnp.concatenate([weights[(e, *lanes)], weights[(e + 1, *lanes)]], axis=1)
        here = jnp.dot(rows, pair, preferred_element_type=F32)
        here = jnp.where(slot % 2 == 0, here[:, :HALF], here[:, HALF:])
        out = here if e == 0 else jnp.where(slot >= e, here, out)
    return out


def first_kernel(own_ref, w_in, pre_ref):
    pre_ref[...] = own_expert(own_ref[...], w_in, (columns(0), slice(None)))


def second_kernel(pre_ref, oth_ref, w_in, w_out, hidden_ref, send_ref):
    value = pre_ref[...] + own_expert(oth_ref[...], w_in, (columns(1), slice(None)))
    hidden_ref[...] = (0.5 * value * (1.0 + lax.erf(value * np.float32(np.sqrt(0.5))))).astype(BF16)
    send_ref[...] = own_expert(hidden_ref[...], w_out, (slice(None), columns(1))).astype(BF16)


def third_kernel(hidden_ref, w_out, keep_ref):
    keep_ref[...] = own_expert(hidden_ref[...], w_out, (slice(None), columns(0)))


def stage(kernel, name, outs, *operands):
    return pl.pallas_call(
        kernel,
        out_shape=outs,
        compiler_params=pltpu.CompilerParams(vmem_limit_bytes=24 << 20),
        cost_estimate=pl.CostEstimate(
            flops=128 * sum(x.size for x in operands), bytes_accessed=2 * sum(x.size for x in operands), transcendentals=0
        ),
        name=name,
    )(*operands)


def combine_kernel(logits_ref, out_ref):
    for b in range(2):
        logits = logits_ref[b]
        expd = jnp.exp(logits - jnp.max(logits, axis=0, keepdims=True))
        combine = expd / jnp.sum(expd, axis=0, keepdims=True)
        out_ref[b] = combine.T.astype(BF16)


def combine(logits):
    clips, slots, count = logits.shape
    return pl.pallas_call(
        combine_kernel,
        out_shape=jax.ShapeDtypeStruct((clips, count, slots), BF16),
        compiler_params=pltpu.CompilerParams(vmem_limit_bytes=24 << 20),
        cost_estimate=pl.CostEstimate(flops=8 * logits.size, bytes_accessed=6 * logits.size, transcendentals=logits.size),
        name="combine",
    )(logits)


def sum_kernel(parts_ref, out_ref):
    row = lax.broadcasted_iota(jnp.int32, (128, 512), 0)
    part = lax.broadcasted_iota(jnp.int32, (128, 512), 1)
    same = ((row // 64) * 4 + row % 4 == part % 8) & ((row % 64) // 4 == part // 32)
    ones = jnp.where(same, 1.0, 0.0).astype(BF16)
    total = jnp.dot(ones, parts_ref[...].reshape(512, HALF), preferred_element_type=F32)
    out_ref[...] = total.astype(BF16).reshape(2, 64, HALF)


def sum_parts(parts):
    return pl.pallas_call(
        sum_kernel,
        out_shape=jax.ShapeDtypeStruct((2, 64, HALF), BF16),
        compiler_params=pltpu.CompilerParams(vmem_limit_bytes=24 << 20),
        name="sum_parts",
    )(parts)


def mix_own_kernel(early, combine_ref, own_ref, out_hbm, held_ref, sem):
    clips, count, _ = held_ref.shape
    rows = pl.ds(0, early)
    held_ref[0, rows] = jnp.dot(combine_ref[0, rows], own_ref[0], preferred_element_type=F32).astype(BF16)
    copy = pltpu.make_async_copy(held_ref.at[0, rows], out_hbm.at[0, rows, columns(0)], sem)
    copy.start()
    rows = pl.ds(early, count - early)
    held_ref[0, rows] = jnp.dot(combine_ref[0, rows], own_ref[0], preferred_element_type=F32).astype(BF16)
    for b in range(1, clips):
        held_ref[b] = jnp.dot(combine_ref[b], own_ref[b], preferred_element_type=F32).astype(BF16)
    copy.wait()


def mix_own(weights, own):
    clips, count, _ = weights.shape
    vmem = pl.BlockSpec(memory_space=pltpu.VMEM)
    return pl.pallas_call(
        functools.partial(mix_own_kernel, EARLY),
        out_shape=[
            jax.ShapeDtypeStruct((clips, count, 2 * HALF), BF16),
            pltpu.VMEM((clips, count, HALF), BF16),
        ],
        in_specs=[vmem] * 2,
        out_specs=[pl.BlockSpec(memory_space=pl.ANY), vmem],
        scratch_shapes=[pltpu.SemaphoreType.DMA(())],
        compiler_params=pltpu.CompilerParams(vmem_limit_bytes=24 << 20),
        cost_estimate=pl.CostEstimate(
            flops=2 * weights.size * HALF, bytes_accessed=2 * clips * count * HALF, transcendentals=0
        ),
        name="mix_own",
    )(weights, own)


def mix_kernel(pieces, early, combine_ref, oth_ref, held_ref, _, out_hbm, mixed, sems):
    clips, count, _ = mixed.shape
    copies = []
    for b in range(clips):
        first = early if b == 0 else 0
        rows = pl.ds(first, count - first)
        copies.append(pltpu.make_async_copy(held_ref.at[b, rows], out_hbm.at[b, rows, columns(0)], sems.at[clips, b]))
        copies[-1].start()
    for b in range(clips):
        for i in range(pieces):
            rows = pl.ds(i * (count // pieces), count // pieces)
            mixed[b, rows] = jnp.dot(combine_ref[b, rows], oth_ref[b], preferred_element_type=F32).astype(BF16)
            copies.append(pltpu.make_async_copy(mixed.at[b, rows], out_hbm.at[b, rows, columns(1)], sems.at[b, i]))
            copies[-1].start()
    for copy in copies:
        copy.wait()


def mix(weights, oth, held, out):
    clips, count, _ = weights.shape
    pieces = 2
    vmem, hbm = pl.BlockSpec(memory_space=pltpu.VMEM), pl.BlockSpec(memory_space=pl.ANY)
    return pl.pallas_call(
        functools.partial(mix_kernel, pieces, EARLY),
        out_shape=jax.ShapeDtypeStruct(out.shape, BF16),
        in_specs=[vmem] * 3 + [hbm],
        out_specs=hbm,
        scratch_shapes=[pltpu.VMEM((clips, count, HALF), BF16), pltpu.SemaphoreType.DMA((clips + 1, pieces))],
        input_output_aliases={3: 0},
        compiler_params=pltpu.CompilerParams(vmem_limit_bytes=32 << 20),
        name="mix",
    )(weights, oth, held, out)


def swap(x):
    return lax.ppermute(x, "core", [(0, 1), (1, 0)])


def exchange(x):
    return lax.all_to_all(x, ("dp", "x"), 0, 0, tiled=True)


def on_device(tokens, slot_param, w_in, w_out):
    send, stats, dispatch, logits, held = gather(
        pltpu.with_memory_space_constraint(tokens, pltpu.HBM),
        pltpu.with_memory_space_constraint(slot_param.T, pltpu.HBM),
    )
    keep, weights = lax.optimization_barrier((keep_half(dispatch, held), combine(logits)))
    own = reduce(exchange(pack(keep, stats, swap(send))))
    pre = stage(first_kernel, "first", pltpu.VMEM((128, HALF), F32), own, w_in)
    outs = [pltpu.VMEM((128, HALF), BF16)] * 2
    hidden, send = stage(second_kernel, "second", outs, pre, swap(own), w_in, w_out)
    keep = stage(third_kernel, "third", pltpu.VMEM((128, HALF), F32), hidden, w_out)
    summed = (keep + swap(send).astype(F32)).astype(BF16).reshape(16, 1, 8, HALF)
    own = sum_parts(exchange(jnp.broadcast_to(summed, (16, 4, 8, HALF)).reshape(64, 8, HALF)))
    out, held = mix_own(weights, own)
    return mix(weights, swap(own), held, out)


def solution(mesh):
    ctx = ("x", "core")
    split = jax.sharding.Mesh(np.asarray(mesh.devices).reshape(16, 4, 2), ("dp",) + ctx)
    placed = (P("dp", ctx, None), P(), P("dp", None, ctx), P("dp", ctx, None))
    return jax.shard_map(
        on_device, mesh=split, in_specs=placed, out_specs=P("dp", ctx, None), check_vma=False
    )
```

```python
import functools

import jax
import jax.numpy as jnp
import numpy as np
from jax import lax
from jax.experimental import pallas as pl
from jax.experimental.pallas import tpu as pltpu
from jax.sharding import PartitionSpec as P

F32 = jnp.float32
BF16 = jnp.bfloat16
HALF = 640
WIDE = HALF + 128
EARLY = 256
NT = (((1,), (1,)), ((), ()))


def columns(half):
    core = lax.axis_index("core")
    return pl.ds(pl.multiple_of((core if half == 0 else 1 - core) * HALF, 128), HALF)


def stats_block(peak, total):
    high = total.astype(BF16).astype(F32)
    lane = lax.broadcasted_iota(jnp.int32, (peak.shape[0], 128), 1)
    return jnp.where(lane == 0, peak, jnp.where(lane == 1, high, jnp.where(lane == 2, total - high, 0.0)))


def gather_kernel(
    pieces, tokens_hbm, slots_hbm, send_ref, stats_ref, dispatch_ref, logits_ref, tokens_ref, slots, sems
):
    clips, count, _ = tokens_ref.shape
    step = count // pieces

    def copy(b, i):
        rows = pl.ds(i * step, step)
        return pltpu.make_async_copy(tokens_hbm.at[b, rows], tokens_ref.at[b, rows], sems.at[b, i])

    slots_copy = pltpu.make_async_copy(slots_hbm, slots, sems.at[clips, 0])
    slots_copy.start()
    for b in range(clips):
        for i in range(pieces):
            copy(b, i).start()
    slots_copy.wait()
    for b in range(clips):
        for i in range(pieces):
            copy(b, i).wait()
            rows = pl.ds(i * step, step)
            logits_ref[b, :, rows] = lax.dot_general(
                slots[...], tokens_ref[b, rows, :], NT, preferred_element_type=F32
            )
    for b in range(clips):
        logits = logits_ref[b]
        peak = jnp.max(logits, axis=1, keepdims=True).astype(BF16).astype(F32)
        expd = jnp.exp(logits - peak)
        stats = stats_block(peak, jnp.sum(expd, axis=1, keepdims=True))
        dispatch_ref[b] = expd.astype(BF16)
        stats_ref[b] = stats
        send_ref[b, :, pl.ds(HALF, 128)] = stats.astype(BF16)
        send_ref[b, :, pl.ds(0, HALF)] = jnp.dot(
            dispatch_ref[b], tokens_ref[b, :, columns(1)], preferred_element_type=F32
        ).astype(BF16)


def gather(tokens, slots_t):
    clips, count, width = tokens.shape
    slots = slots_t.shape[0]
    pieces = 2
    vmem = pl.BlockSpec(memory_space=pltpu.VMEM)
    return pl.pallas_call(
        functools.partial(gather_kernel, pieces),
        out_shape=[
            pltpu.VMEM((clips, slots, WIDE), BF16),
            pltpu.VMEM((clips, slots, 128), F32),
            pltpu.VMEM((clips, slots, count), BF16),
            pltpu.VMEM((clips, slots, count), F32),
            pltpu.VMEM((clips, count, width), BF16),
        ],
        in_specs=[pl.BlockSpec(memory_space=pl.ANY)] * 2,
        out_specs=[vmem] * 5,
        scratch_shapes=[pltpu.VMEM((slots, width), BF16), pltpu.SemaphoreType.DMA((clips + 1, pieces))],
        compiler_params=pltpu.CompilerParams(vmem_limit_bytes=56 << 20),
        cost_estimate=pl.CostEstimate(
            flops=3 * clips * slots * count * width,
            bytes_accessed=2 * clips * count * width,
            transcendentals=clips * slots * count,
        ),
        name="gather",
    )(tokens, slots_t)


def keep_kernel(dispatch_ref, tokens_ref, out_ref):
    for b in range(dispatch_ref.shape[0]):
        out_ref[b] = jnp.dot(dispatch_ref[b], tokens_ref[b, :, columns(0)], preferred_element_type=F32)


def keep_half(dispatch, tokens):
    clips, slots, count = dispatch.shape
    return pl.pallas_call(
        keep_kernel,
        out_shape=pltpu.VMEM((clips, slots, HALF), F32),
        compiler_params=pltpu.CompilerParams(vmem_limit_bytes=16 << 20),
        cost_estimate=pl.CostEstimate(
            flops=2 * clips * slots * count * HALF, bytes_accessed=2 * tokens.size, transcendentals=0
        ),
        name="keep_half",
    )(dispatch, tokens)


def pack_kernel(keep_ref, stats_ref, recv_ref, out_ref):
    halves = []
    for b in range(2):
        kept, stats, got = keep_ref[b], stats_ref[b], recv_ref[b].astype(F32)
        peak_k, peak_g = stats[:, :1], got[:, HALF : HALF + 1]
        peak = jnp.maximum(peak_k, peak_g)
        scale_k, scale_g = jnp.exp(peak_k - peak), jnp.exp(peak_g - peak)
        total = scale_k * (stats[:, 1:2] + stats[:, 2:3]) + scale_g * (
            got[:, HALF + 1 : HALF + 2] + got[:, HALF + 2 : HALF + 3]
        )
        value = scale_k * kept + scale_g * got[:, :HALF]
        halves.append(jnp.concatenate([value, stats_block(peak, total)], axis=1).reshape(8, 8, WIDE))
    first, second = halves
    top = lax.broadcasted_iota(jnp.int32, first.shape, 1) < 4
    even = jnp.where(top, first, pltpu.roll(second, 4, 1)).astype(BF16)
    odd = jnp.where(top, pltpu.roll(first, 4, 1), second).astype(BF16)
    for j in range(8):
        for x in range(4):
            out_ref[8 * j + x] = even[j]
            out_ref[8 * j + 4 + x] = odd[j]


def pack(keep, stats, recv):
    return pl.pallas_call(
        pack_kernel,
        out_shape=jax.ShapeDtypeStruct((64, 8, WIDE), BF16),
        compiler_params=pltpu.CompilerParams(vmem_limit_bytes=24 << 20),
        cost_estimate=pl.CostEstimate(flops=1 << 36, bytes_accessed=100 << 20, transcendentals=0),
        name="pack",
    )(keep, stats, recv)


def reduce_kernel(parts_ref, out_ref):
    stats = parts_ref[:, :, pl.ds(HALF, 128)].astype(F32).reshape(16, 4, 8, 128)
    peak = stats[..., :1]
    weight = jnp.exp(peak - jnp.max(peak, axis=1, keepdims=True))
    total = jnp.sum(weight * (stats[..., 1:2] + stats[..., 2:3]), axis=1, keepdims=True)
    weight = jnp.broadcast_to(weight / total, (16, 4, 8, 128))
    for i in range(8):
        scale = jnp.concatenate([weight[2 * i : 2 * i + 2]] * (HALF // 128), axis=-1)
        part = parts_ref[8 * i : 8 * i + 8, :, pl.ds(0, HALF)].astype(F32).reshape(2, 4, 8, HALF)
        out_ref[pl.ds(16 * i, 16), :] = jnp.sum(scale * part, axis=1).reshape(16, HALF).astype(BF16)


def reduce(parts):
    return pl.pallas_call(
        reduce_kernel,
        out_shape=jax.ShapeDtypeStruct((128, HALF), BF16),
        compiler_params=pltpu.CompilerParams(vmem_limit_bytes=24 << 20),
        name="reduce",
    )(parts)


def own_expert(rows, weights, lanes):
    experts = weights.shape[0]
    slot = lax.broadcasted_iota(jnp.int32, (rows.shape[0], 1), 0) % experts
    out = None
    for e in range(0, experts, 2):
        pair = jnp.concatenate([weights[(e, *lanes)], weights[(e + 1, *lanes)]], axis=1)
        here = jnp.dot(rows, pair, preferred_element_type=F32)
        here = jnp.where(slot % 2 == 0, here[:, :HALF], here[:, HALF:])
        out = here if e == 0 else jnp.where(slot >= e, here, out)
    return out


def first_kernel(own_ref, w_in, pre_ref):
    pre_ref[...] = own_expert(own_ref[...], w_in, (columns(0), slice(None)))


def second_kernel(pre_ref, oth_ref, w_in, w_out, hidden_ref, send_ref):
    value = pre_ref[...] + own_expert(oth_ref[...], w_in, (columns(1), slice(None)))
    hidden_ref[...] = (0.5 * value * (1.0 + lax.erf(value * np.float32(np.sqrt(0.5))))).astype(BF16)
    send_ref[...] = own_expert(hidden_ref[...], w_out, (slice(None), columns(1))).astype(BF16)


def third_kernel(hidden_ref, w_out, keep_ref):
    keep_ref[...] = own_expert(hidden_ref[...], w_out, (slice(None), columns(0)))


def stage(kernel, name, outs, *operands):
    return pl.pallas_call(
        kernel,
        out_shape=outs,
        compiler_params=pltpu.CompilerParams(vmem_limit_bytes=24 << 20),
        cost_estimate=pl.CostEstimate(
            flops=128 * sum(x.size for x in operands), bytes_accessed=2 * sum(x.size for x in operands), transcendentals=0
        ),
        name=name,
    )(*operands)


def combine_kernel(logits_ref, out_ref):
    for b in range(2):
        logits = logits_ref[b]
        expd = jnp.exp(logits - jnp.max(logits, axis=0, keepdims=True))
        combine = expd / jnp.sum(expd, axis=0, keepdims=True)
        out_ref[b] = combine.T.astype(BF16)


def combine(logits):
    clips, slots, count = logits.shape
    return pl.pallas_call(
        combine_kernel,
        out_shape=jax.ShapeDtypeStruct((clips, count, slots), BF16),
        compiler_params=pltpu.CompilerParams(vmem_limit_bytes=24 << 20),
        cost_estimate=pl.CostEstimate(flops=8 * logits.size, bytes_accessed=6 * logits.size, transcendentals=logits.size),
        name="combine",
    )(logits)


def sum_kernel(parts_ref, out_ref):
    row = lax.broadcasted_iota(jnp.int32, (128, 512), 0)
    part = lax.broadcasted_iota(jnp.int32, (128, 512), 1)
    same = ((row // 64) * 4 + row % 4 == part % 8) & ((row % 64) // 4 == part // 32)
    ones = jnp.where(same, 1.0, 0.0).astype(BF16)
    parts = parts_ref[...].astype(F32).reshape(512, HALF).astype(BF16)
    total = jnp.dot(ones, parts, preferred_element_type=F32)
    out_ref[...] = total.astype(BF16).reshape(2, 64, HALF)


def sum_parts(parts):
    return pl.pallas_call(
        sum_kernel,
        out_shape=jax.ShapeDtypeStruct((2, 64, HALF), BF16),
        compiler_params=pltpu.CompilerParams(vmem_limit_bytes=24 << 20),
        name="sum_parts",
    )(parts)


def mix_own_kernel(early, combine_ref, own_ref, out_hbm, held_ref, sem):
    clips, count, _ = held_ref.shape
    rows = pl.ds(0, early)
    held_ref[0, rows] = jnp.dot(combine_ref[0, rows], own_ref[0], preferred_element_type=F32).astype(BF16)
    copy = pltpu.make_async_copy(held_ref.at[0, rows], out_hbm.at[0, rows, columns(0)], sem)
    copy.start()
    rows = pl.ds(early, count - early)
    held_ref[0, rows] = jnp.dot(combine_ref[0, rows], own_ref[0], preferred_element_type=F32).astype(BF16)
    for b in range(1, clips):
        held_ref[b] = jnp.dot(combine_ref[b], own_ref[b], preferred_element_type=F32).astype(BF16)
    copy.wait()


def mix_own(weights, own):
    clips, count, _ = weights.shape
    vmem = pl.BlockSpec(memory_space=pltpu.VMEM)
    return pl.pallas_call(
        functools.partial(mix_own_kernel, EARLY),
        out_shape=[
            jax.ShapeDtypeStruct((clips, count, 2 * HALF), BF16),
            pltpu.VMEM((clips, count, HALF), BF16),
        ],
        in_specs=[vmem] * 2,
        out_specs=[pl.BlockSpec(memory_space=pl.ANY), vmem],
        scratch_shapes=[pltpu.SemaphoreType.DMA(())],
        compiler_params=pltpu.CompilerParams(vmem_limit_bytes=24 << 20),
        cost_estimate=pl.CostEstimate(
            flops=2 * weights.size * HALF, bytes_accessed=2 * clips * count * HALF, transcendentals=0
        ),
        name="mix_own",
    )(weights, own)


def mix_kernel(pieces, early, combine_ref, oth_ref, held_ref, _, out_hbm, mixed, sems):
    clips, count, _ = mixed.shape
    copies = []
    for b in range(clips):
        first = early if b == 0 else 0
        rows = pl.ds(first, count - first)
        copies.append(pltpu.make_async_copy(held_ref.at[b, rows], out_hbm.at[b, rows, columns(0)], sems.at[clips, b]))
        copies[-1].start()
    for b in range(clips):
        for i in range(pieces):
            rows = pl.ds(i * (count // pieces), count // pieces)
            mixed[b, rows] = jnp.dot(combine_ref[b, rows], oth_ref[b], preferred_element_type=F32).astype(BF16)
            copies.append(pltpu.make_async_copy(mixed.at[b, rows], out_hbm.at[b, rows, columns(1)], sems.at[b, i]))
            copies[-1].start()
    for copy in copies:
        copy.wait()


def mix(weights, oth, held, out):
    clips, count, _ = weights.shape
    pieces = 2
    vmem, hbm = pl.BlockSpec(memory_space=pltpu.VMEM), pl.BlockSpec(memory_space=pl.ANY)
    return pl.pallas_call(
        functools.partial(mix_kernel, pieces, EARLY),
        out_shape=jax.ShapeDtypeStruct(out.shape, BF16),
        in_specs=[vmem] * 3 + [hbm],
        out_specs=hbm,
        scratch_shapes=[pltpu.VMEM((clips, count, HALF), BF16), pltpu.SemaphoreType.DMA((clips + 1, pieces))],
        input_output_aliases={3: 0},
        compiler_params=pltpu.CompilerParams(vmem_limit_bytes=32 << 20),
        name="mix",
    )(weights, oth, held, out)


def swap(x):
    return lax.ppermute(x, "core", [(0, 1), (1, 0)])


def exchange(x):
    return lax.all_to_all(x, ("dp", "x"), 0, 0, tiled=True)


def on_device(tokens, slot_param, w_in, w_out):
    send, stats, dispatch, logits, held = gather(
        pltpu.with_memory_space_constraint(tokens, pltpu.HBM),
        pltpu.with_memory_space_constraint(slot_param.T, pltpu.HBM),
    )
    keep, weights = lax.optimization_barrier((keep_half(dispatch, held), combine(logits)))
    own = reduce(exchange(pack(keep, stats, swap(send))))
    pre = stage(first_kernel, "first", pltpu.VMEM((128, HALF), F32), own, w_in)
    outs = [pltpu.VMEM((128, HALF), BF16)] * 2
    hidden, send = stage(second_kernel, "second", outs, pre, swap(own), w_in, w_out)
    keep = stage(third_kernel, "third", pltpu.VMEM((128, HALF), F32), hidden, w_out)
    summed = (keep + swap(send).astype(F32)).astype(BF16).reshape(16, 1, 8, HALF)
    own = sum_parts(exchange(jnp.broadcast_to(summed, (16, 4, 8, HALF)).reshape(64, 8, HALF)))
    out, held = mix_own(weights, own)
    return mix(weights, swap(own), held, out)


def solution(mesh):
    ctx = ("x", "core")
    split = jax.sharding.Mesh(np.asarray(mesh.devices).reshape(16, 4, 2), ("dp",) + ctx)
    placed = (P("dp", ctx, None), P(), P("dp", None, ctx), P("dp", ctx, None))
    return jax.shard_map(
        on_device, mesh=split, in_specs=placed, out_specs=P("dp", ctx, None), check_vma=False
    )
```
